32 devices in a mesh: groups: 2 (over y), strip: 4 (over z), sub: 2 (over x), rep: 2 (over core).
Axes of the slice: x: 2, y: 2, z: 4, core: 2. Of those that a mesh axis runs over, the one named last changes fastest.
Arguments:
- source: bfloat16 [32, 16, 128, 128], P(('groups', 'strip'), 'sub', 'rep'), parts along dimension 0, may hold values from -6 to 6
- target: bfloat16 [32, 16, 128, 128], P(('groups', 'strip'), 'sub', 'rep'), parts along dimension 0, may hold values from -6 to 6
- target_ids: int32 [32, 16, 25], P(('groups', 'strip'), 'sub'), parts along dimension 0, may hold values from 0 to 255, as said below
- out_grad: bfloat16 [32, 16, 25, 128], P(('groups', 'strip'), 'sub'), parts along dimension 0, may hold values from -6 to 6
- w_in: bfloat16 [128, 256], replicated, may hold values from -0.5 to 0.5
- b_in: float32 [256], replicated, may hold values from -4 to 4
- w_out: bfloat16 [256, 128], replicated, may hold values from -0.375 to 0.375
Outputs:
- source_grad: bfloat16 [32, 16, 128, 128], P(('groups', 'strip'), 'sub', 'rep'), parts along dimension 0
- target_grad: bfloat16 [32, 16, 128, 128], P(('groups', 'strip'), 'sub', 'rep'), parts along dimension 0
The draws below stay inside these ranges and needn't reach their ends.
There are 2 independent parts, one for each index of `groups`. The reference program is written for one: setup_inputs(seed, part) draws one part's arguments, and reference() takes and returns one part's arrays. A program takes and returns all parts, laid end to end along the dimension named above; an argument that names none is the same for every part. Nothing has to cross between parts.
Inputs may be any that keep to these rules, and one draw needn't show every extreme that they name: `target_ids`: the targets of source block (i, j) lie within 3 block rows and 3 block columns of it and inside the section; they come in no particular order and may repeat.
All inputs are finite; a program needn't handle non-finite values.
Results may differ from the reference program's by a relative error of at most 0.007.
Values may be sent and summed in bfloat16 or wider, within the bound.
A program may use at most 64 MiB of HBM per device.

```python
import math
import jax
import jax.numpy as jnp
from jax import lax

C = 128
P_SIZE = 128
HID = 256
K = 25
H = 3
NBR = 16
NBC = 16


def draw_target_ids(key, part):
    row_key = jax.random.fold_in(key, 11)
    col_key = jax.random.fold_in(key, 12)
    row_move = jax.random.randint(row_key, (NBR, NBC, K), -H, H + 1)
    col_move = jax.random.randint(col_key, (NBR, NBC, K), -H, H + 1)
    row_at = jnp.arange(NBR, dtype=jnp.int32)[:, None, None]
    col_at = jnp.arange(NBC, dtype=jnp.int32)[None, :, None]
    target_row = jnp.clip(row_at + row_move, 0, NBR - 1)
    target_col = jnp.clip(col_at + col_move, 0, NBC - 1)
    return (target_row * NBC + target_col).astype(jnp.int32)


def level_of(rng, dims, cuts, smallest, top_value):
    def one(dim, shards_of):
        draws = jax.random.uniform(jax.random.fold_in(jax.random.fold_in(rng, 6), dim), (shards_of,), jnp.float32, smallest / len(cuts), top_value / len(cuts))
        return jnp.repeat(jnp.exp(draws), dims[dim] // shards_of).reshape((-1,) + (1,) * (len(dims) - dim - 1))

    gain = one(*cuts[0])
    for cut in cuts[1:]:
        gain = gain * one(*cut)
    return gain


def centred(key, extent, deviation, reach, pieces=(), kind=jnp.bfloat16):
    level = level_of(key, extent, pieces, -0.22, 0.18) if pieces else 1.0
    array = jax.random.normal(key, extent, jnp.float32) * deviation * level
    return jnp.minimum(jnp.maximum(array, -reach), reach).astype(kind)


def setup_inputs(seed: int = 0, part: int = 0) -> dict:
    splits = jax.random.split(jax.random.key(seed), 8)
    part_keys = jax.random.split(jax.random.fold_in(splits[7], part), 8)
    source = centred(part_keys[0], (NBR, NBC, P_SIZE, C), 1.0, 6.0, ((0, 4), (1, 2), (2, 2)))
    target = centred(part_keys[1], (NBR, NBC, P_SIZE, C), 1.0, 6.0, ((0, 4), (1, 2), (2, 2)))
    target_ids = draw_target_ids(jax.random.fold_in(jax.random.fold_in(splits[7], part), 71), part)
    out_grad = centred(part_keys[3], (NBR, NBC, K, P_SIZE), 1.0, 6.0, ((0, 4), (1, 2)))
    w_in = centred(splits[4], (P_SIZE, HID), P_SIZE ** -0.5, 0.5)
    b_in = centred(splits[5], (HID,), 1.0, 4.0, (), jnp.float32)
    w_out = centred(splits[6], (HID, P_SIZE), HID ** -0.5, 0.375)
    return {"source": source, "target": target, "target_ids": target_ids, "out_grad": out_grad, "w_in": w_in, "b_in": b_in, "w_out": w_out}


def gelu_tanh(values):
    return jax.nn.gelu(values, approximate=True)

def reference(source, target, target_ids, out_grad, w_in, b_in, w_out):
    inv_root = 1.0 / math.sqrt(C)
    flat_target = target.reshape(NBR * NBC, P_SIZE, C)

    def row_costs(items):
        src_row, id_row = items
        chosen = flat_target[id_row.astype(jnp.int32)]
        total = jnp.einsum('jpc,jkpc->jkp', src_row.astype(jnp.float32), chosen.astype(jnp.float32))
        return (total * inv_root).astype(jnp.bfloat16)
    costs = lax.map(row_costs, (source, target_ids))
    cost_rows = costs.reshape(-1, P_SIZE)
    hidden_pre = jnp.dot(cost_rows, w_in, preferred_element_type=jnp.float32) + b_in.astype(jnp.float32)
    grad_hidden = lax.dot_general(out_grad.reshape(-1, P_SIZE), w_out, (((1,), (1,)), ((), ())), preferred_element_type=jnp.float32)
    _, pullback = jax.vjp(gelu_tanh, hidden_pre)
    grad_pre = pullback(grad_hidden)[0].astype(jnp.bfloat16)
    grad_cost = lax.dot_general(grad_pre, w_in, (((1,), (1,)), ((), ())), preferred_element_type=jnp.float32)
    grad_cost = grad_cost.astype(jnp.bfloat16).reshape(NBR, NBC, K, P_SIZE)
    same_id = target_ids[..., :, None] == target_ids[..., None, :]
    merged = jnp.einsum('ijkl,ijlp->ijkp', same_id.astype(jnp.float32), grad_cost.astype(jnp.float32)).astype(jnp.bfloat16)
    earlier = jnp.arange(K)[None, :] < jnp.arange(K)[:, None]
    first = jnp.logical_not(jnp.any(same_id & earlier, axis=-1))
    weights = merged.astype(jnp.float32) * first[..., None].astype(jnp.float32)

    def row_grads(accum, items):
        src_row, id_row, wgt_row = items
        chosen = flat_target[id_row.astype(jnp.int32)].astype(jnp.float32)
        src_grad = (jnp.einsum('jkp,jkpc->jpc', wgt_row, chosen) * inv_root).astype(jnp.bfloat16)
        contrib = wgt_row[..., None] * src_row.astype(jnp.float32)[:, None]
        accum = accum.at[id_row.reshape(-1).astype(jnp.int32)].add(contrib.reshape(-1, P_SIZE, C))
        return (accum, src_grad)
    accum_start = jnp.zeros((NBR * NBC, P_SIZE, C), jnp.float32)
    accum, source_grad = lax.scan(row_grads, accum_start, (source, target_ids, weights))
    target_grad = (accum * inv_root).astype(jnp.bfloat16).reshape(NBR, NBC, P_SIZE, C)
    return (source_grad, target_grad)
```

```python
from functools import partial
import math

import jax
import jax.numpy as jnp
from jax import lax
from jax.experimental import pallas as pl
from jax.experimental.pallas import tpu as pltpu
from jax.sharding import PartitionSpec as P

H = 3
MESH = pl.DeviceIdType.MESH
DIRS = ((-1, 0), (1, 0), (0, -1), (0, 1), (-1, -1), (-1, 1), (1, -1), (1, 1))
ROW_STEP = 4096
F32 = jnp.float32
BF16 = jnp.bfloat16
NT = (((1,), (1,)), ((), ()))


def gelu_slope(x):
    a = math.sqrt(2.0 / math.pi)
    x2 = x * x
    t = jnp.tanh(a * x * (1.0 + 0.044715 * x2))
    return 0.5 * (1.0 + t) + (0.5 * a) * x * (1.0 - t * t) * (1.0 + (3 * 0.044715) * x2)


def cut(step, count, width, lead):
    if step < 0:
        return 0, width, lead + count
    if step > 0:
        return count - width, width, lead - width
    return 0, count, lead


def kernel(cfg, src_ref, tgt_ref, code_ref, og_ref, win_ref, bin_ref, wout_ref,
           sg_ref, tg_ref,
           t_ext, s_ext, t32, s32, corr32, pw32, pwx32, oh_e, oh_m, gh, cst, gc, gext,
           cx, out32, send_sem, recv_sem, local_sem, rep_sem):
    R, CB, PH, C, K, KP, ns, nc = cfg
    J = 128 // KP
    NG = CB // J
    NB = R * CB
    ER, EC = R + 2 * H, CB + 2 * H
    E = ER * EC
    EP = t32.shape[0] // PH
    GC = NG + 2
    SC = GC * J
    G = ER * GC
    HID = win_ref.shape[1]
    inv_root = 1.0 / math.sqrt(C)

    z = lax.axis_index("strip")
    x = lax.axis_index("sub")
    rep = lax.axis_index("rep")
    other = 1 - rep

    def exists(dr, dc):
        ok = jnp.bool_(True)
        if dr < 0:
            ok = jnp.logical_and(ok, z > 0)
        if dr > 0:
            ok = jnp.logical_and(ok, z < ns - 1)
        if dc < 0:
            ok = jnp.logical_and(ok, x > 0)
        if dc > 0:
            ok = jnp.logical_and(ok, x < nc - 1)
        return ok

    def device(dr, dc):
        return {"strip": z + dr, "sub": x + dc}

    barrier = pltpu.get_barrier_semaphore()
    for dr, dc in DIRS:
        @pl.when(exists(dr, dc))
        def _():
            pl.semaphore_signal(barrier, inc=1, device_id=device(dr, dc), device_id_type=MESH)
    pl.semaphore_signal(barrier, inc=1, device_id={"rep": other}, device_id_type=MESH)
    own_t = pltpu.make_async_copy(tgt_ref, t_ext.at[pl.ds(H, R), pl.ds(H, CB)], local_sem.at[0])
    own_t.start()
    own_s = pltpu.make_async_copy(src_ref, s_ext.at[pl.ds(H, R), pl.ds(J, CB)], local_sem.at[1])
    own_s.start()
    rows_n = 1 + (z > 0).astype(jnp.int32) + (z < ns - 1).astype(jnp.int32)
    cols_n = 1 + (x > 0).astype(jnp.int32) + (x < nc - 1).astype(jnp.int32)
    pl.semaphore_wait(barrier, rows_n * cols_n)

    def copy_of(what, d):
        dr, dc = DIRS[d]
        r0, rn, rd = cut(dr, R, H, H)
        if what == 0:
            c0, cn, cd = cut(dc, CB, H, H)
            a, b = tgt_ref.at[pl.ds(r0, rn), pl.ds(c0, cn)], t_ext.at[pl.ds(rd, rn), pl.ds(cd, cn)]
        elif what == 1:
            c0, cn, cd = cut(dc, CB, H, J)
            a, b = src_ref.at[pl.ds(r0, rn), pl.ds(c0, cn)], s_ext.at[pl.ds(rd, rn), pl.ds(cd, cn)]
        elif what == 2:
            a, b = code_ref, cx.at[d]
        else:
            c0, cn, cd = cut(dc, NG, 1, 1)
            a, b = gc.at[pl.ds(r0, rn), pl.ds(c0, cn)], gext.at[pl.ds(rd, rn), pl.ds(cd, cn)]
        return pltpu.make_async_remote_copy(
            src_ref=a, dst_ref=b, send_sem=send_sem.at[what, d], recv_sem=recv_sem.at[what, d],
            device_id=device(dr, dc), device_id_type=MESH)

    def start(what):
        for d, (dr, dc) in enumerate(DIRS):
            @pl.when(exists(dr, dc))
            def _():
                copy_of(what, d).start()

    def wait_send(what):
        for d, (dr, dc) in enumerate(DIRS):
            @pl.when(exists(dr, dc))
            def _():
                copy_of(what, d).wait_send()

    def wait_recv(what):
        for d, (dr, dc) in enumerate(DIRS):
            @pl.when(exists(-dr, -dc))
            def _():
                copy_of(what, d).wait_recv()

    start(2)
    start(0)

    for d, (dr, dc) in enumerate(DIRS):
        @pl.when(jnp.logical_not(exists(-dr, -dc)))
        def _():
            _, rn, rd = cut(dr, R, H, H)
            _, cn, cd = cut(dc, CB, H, H)
            t_ext[pl.ds(rd, rn), pl.ds(cd, cn)] = jnp.zeros((rn, cn, PH, C), BF16)
            _, cn, cd = cut(dc, CB, H, J)
            s_ext[pl.ds(rd, rn), pl.ds(cd, cn)] = jnp.zeros((rn, cn, PH, C), BF16)
            _, cn, cd = cut(dc, NG, 1, 1)
            gext[pl.ds(rd, rn), pl.ds(cd, cn)] = jnp.zeros((rn, cn, PH, J * KP), BF16)
            cx[d] = jnp.full((R, 8, J * KP), 1 << 30, jnp.int32)
    for c in tuple(range(J - H)) + tuple(range(J + CB + H, SC)):
        s_ext[:, c] = jnp.zeros((ER, PH, C), BF16)
    if EP > E:
        t32[pl.ds(E * PH, (EP - E) * PH), :] = jnp.zeros(((EP - E) * PH, C), F32)

    gh[...] = jnp.zeros_like(gh)
    for b in range(NB):
        gh[pl.ds(b * KP, K), :] = lax.dot_general(
            og_ref[b], wout_ref[...], NT, preferred_element_type=F32)

    code_own = code_ref[...].reshape(R * 8, J * KP).T
    lane_e = lax.broadcasted_iota(jnp.int32, (J * KP, EP), 1)
    for r in range(R):
        for h in range(NG):
            col = code_own[:, r * 8 + h:r * 8 + h + 1]
            e = ((col >> 12) - z * R + H) * EC + (col & (ROW_STEP - 1)) - x * CB + H
            oh_e[r * NG + h] = jnp.where(lane_e == e, 1.0, 0.0).astype(BF16)

    wait_recv(2)
    lane_m = lax.broadcasted_iota(jnp.int32, (J * KP, J * NB), 1)
    seat = (lax.broadcasted_iota(jnp.int32, (J * KP, 1), 0) // KP) * NB

    def mark(code_t, r, h, g):
        col = code_t[:, r * 8 + h:r * 8 + h + 1]
        row_m = (col >> 12) - z * R
        col_m = (col & (ROW_STEP - 1)) - x * CB
        inside = (row_m >= 0) & (row_m < R) & (col_m >= 0) & (col_m < CB)
        m = jnp.where(inside, row_m * CB + col_m + seat, -1)
        oh_m[g] = jnp.where(lane_m == m, 1.0, 0.0).astype(BF16)

    for r in range(R):
        for h in range(NG):
            mark(code_own, r, h, (H + r) * GC + 1 + h)
    for d, (dr, dc) in enumerate(DIRS):
        code_t = cx[d].reshape(R * 8, J * KP).T
        r0, rn, rd = cut(dr, R, H, H)
        c0, cn, cd = cut(dc, NG, 1, 1)
        for r in range(rn):
            for h in range(cn):
                mark(code_t, r0 + r, c0 + h, (rd + r) * GC + cd + h)

    own_t.wait()
    own_s.wait()
    wait_send(0)
    start(1)
    wait_recv(0)

    def widen_t(r, _):
        at = pl.multiple_of(r * (EC * PH), EC * PH)
        t32[pl.ds(at, EC * PH), :] = t_ext[r].reshape(EC * PH, C).astype(F32)
        return 0

    lax.fori_loop(0, ER, widen_t, 0)

    def widen_own(r, _):
        at = pl.multiple_of(r * (CB * PH), CB * PH)
        out32[pl.ds(at, CB * PH), :] = s_ext[H + r, pl.ds(J, CB)].reshape(CB * PH, C).astype(F32)
        return 0

    lax.fori_loop(0, R, widen_own, 0)

    def corr_step(p, _):
        s = out32[pl.ds(p, NB, stride=PH), :].astype(BF16)
        t = t32[pl.ds(p, EP, stride=PH), :].astype(BF16)
        full = lax.dot_general(s, t, NT, preferred_element_type=F32) * inv_root
        at = pl.ds(pl.multiple_of(p * NB, NB), NB)
        corr32[0, at, :] = full[:, :128]
        corr32[1, at, :EP - 128] = full[:, 128:]
        return 0

    lax.fori_loop(0, PH, corr_step, 0, unroll=4)

    for b in range(NB):
        at = pl.ds(b, PH, stride=NB)
        lo = corr32[0, at, :].astype(BF16)
        hi = corr32[1, at, :][:, :EP - 128].astype(BF16)
        oh = oh_e[b // J, pl.ds((b % J) * KP, KP), :]
        got = lax.dot_general(oh[:, :128], lo, NT, preferred_element_type=F32)
        got = got + lax.dot_general(oh[:, 128:], hi, NT, preferred_element_type=F32)
        cst[0, pl.ds(b * KP, KP), :] = got.astype(BF16)

    swap = pltpu.make_async_remote_copy(
        src_ref=cst.at[0], dst_ref=cst.at[1], send_sem=rep_sem.at[0], recv_sem=rep_sem.at[1],
        device_id={"rep": other}, device_id_type=MESH)
    swap.start()
    w_mine = win_ref[pl.ds(pl.multiple_of(rep * PH, PH), PH), :]
    w_other = win_ref[pl.ds(pl.multiple_of(other * PH, PH), PH), :]
    swap.wait()

    for r in range(R):
        for h in range(NG):
            at = pl.ds((r * NG + h) * J * KP, J * KP)
            pre = jnp.dot(cst[0, at, :], w_mine, preferred_element_type=F32)
            pre = pre + jnp.dot(cst[1, at, :], w_other, preferred_element_type=F32) + bin_ref[...]
            grad_pre = (gh[at, :] * gelu_slope(pre)).astype(BF16)
            gc[r, h] = lax.dot_general(
                w_mine, grad_pre, NT, preferred_element_type=F32).astype(BF16)
    start(3)

    lane_j = lax.broadcasted_iota(jnp.int32, (PH, J * KP), 1) // KP
    for g in range(R * NG):
        part = gc[g // NG, g % NG]
        stacked = jnp.concatenate(
            [jnp.where(lane_j == j, part, jnp.zeros_like(part)) for j in range(J)], axis=0)
        pw = jnp.dot(stacked, oh_e[g], preferred_element_type=F32).astype(BF16).astype(F32)
        for j in range(J):
            rows = pl.ds(g * J + j, PH, stride=NB)
            piece = pw[j * PH:(j + 1) * PH]
            pw32[0, rows, :] = piece[:, :128]
            pw32[1, rows, :] = jnp.concatenate(
                [piece[:, 128:], jnp.zeros((PH, 256 - EP), F32)], axis=1)

    def source_step(p, _):
        at = pl.ds(pl.multiple_of(p * NB, NB), NB)
        lo = pw32[0, at, :].astype(BF16)
        hi = pw32[1, at, :][:, :EP - 128].astype(BF16)
        t = t32[pl.ds(p, EP, stride=PH), :].astype(BF16)
        out = jnp.dot(lo, t[:128], preferred_element_type=F32)
        out = out + jnp.dot(hi, t[128:], preferred_element_type=F32)
        out32[pl.ds(p, NB, stride=PH), :] = out * inv_root
        return 0

    lax.fori_loop(0, PH, source_step, 0, unroll=4)
    sg_ref[...] = out32[...].astype(BF16).reshape(sg_ref.shape)

    wait_recv(1)

    def widen_s(r, _):
        at = pl.multiple_of(r * (SC * PH), SC * PH)
        s32[pl.ds(at, SC * PH), :] = s_ext[r].reshape(SC * PH, C).astype(F32)
        return 0

    lax.fori_loop(0, ER, widen_s, 0)

    gext[pl.ds(H, R), pl.ds(1, NG)] = gc[...]
    wait_recv(3)
    for g in range(G):
        pwx = jnp.dot(gext[g // GC, g % GC], oh_m[g], preferred_element_type=F32)
        pwx32[pl.ds(g, PH, stride=G), :] = pwx.astype(BF16).astype(F32)

    def target_step(p, _):
        w = pwx32[pl.ds(pl.multiple_of(p * G, G), G), :].T.astype(BF16)
        out = jnp.zeros((NB, C), F32)
        for j in range(J):
            s = s32[pl.ds(j * PH + p, G, stride=J * PH), :].astype(BF16)
            out = out + jnp.dot(w[j * NB:(j + 1) * NB], s, preferred_element_type=F32)
        out32[pl.ds(p, NB, stride=PH), :] = out * inv_root
        return 0

    lax.fori_loop(0, PH, target_step, 0, unroll=4)
    tg_ref[...] = out32[...].astype(BF16).reshape(tg_ref.shape)

    wait_send(1)
    wait_send(2)
    wait_send(3)


def shards(ns, nc, source, target, target_ids, out_grad, w_in, b_in, w_out):
    R, CB, PH, C = source.shape
    K = target_ids.shape[2]
    KP = 32
    J = 128 // KP
    NG = CB // J
    NB = R * CB
    HID = w_in.shape[1]
    ER, EC = R + 2 * H, CB + 2 * H
    E = ER * EC
    EP = -(-E // 16) * 16
    GC = NG + 2
    SC = GC * J
    G = ER * GC
    total_cols = CB * nc
    code = (target_ids // total_cols) * ROW_STEP + target_ids % total_cols
    code = jnp.pad(code, ((0, 0), (0, 0), (0, KP - K)), constant_values=1 << 30)
    code = jnp.pad(code.reshape(R, NG, J * KP), ((0, 0), (0, 8 - NG), (0, 0)),
                   constant_values=1 << 30)
    vmem = pl.BlockSpec(memory_space=pltpu.VMEM)
    hbm = pl.BlockSpec(memory_space=pl.ANY)
    cfg = (R, CB, PH, C, K, KP, ns, nc)
    return pl.pallas_call(
        partial(kernel, cfg),
        out_shape=(jax.ShapeDtypeStruct(source.shape, BF16), jax.ShapeDtypeStruct(target.shape, BF16)),
        in_specs=[hbm, hbm, vmem, vmem, vmem, vmem, vmem],
        out_specs=(vmem, vmem),
        scratch_shapes=[
            pltpu.VMEM((ER, EC, PH, C), BF16),
            pltpu.VMEM((ER, SC, PH, C), BF16),
            pltpu.VMEM((EP * PH, C), F32),
            pltpu.VMEM((ER * SC * PH, C), F32),
            pltpu.VMEM((2, PH * NB, 128), F32),
            pltpu.VMEM((2, PH * NB, 128), F32),
            pltpu.VMEM((PH * G, J * NB), F32),
            pltpu.VMEM((R * NG, J * KP, EP), BF16),
            pltpu.VMEM((G, J * KP, J * NB), BF16),
            pltpu.VMEM((NB * KP, HID), F32),
            pltpu.VMEM((2, NB * KP, PH), BF16),
            pltpu.VMEM((R, NG, PH, J * KP), BF16),
            pltpu.VMEM((ER, GC, PH, J * KP), BF16),
            pltpu.VMEM((8, R, 8, J * KP), jnp.int32),
            pltpu.VMEM((NB * PH, C), F32),
            pltpu.SemaphoreType.DMA((4, 8)),
            pltpu.SemaphoreType.DMA((4, 8)),
            pltpu.SemaphoreType.DMA((2,)),
            pltpu.SemaphoreType.DMA((2,)),
        ],
        compiler_params=pltpu.CompilerParams(
            collective_id=0, has_side_effects=True, vmem_limit_bytes=56 * 1024 * 1024),
    )(source, target, code, out_grad.reshape(NB, K, out_grad.shape[3]), w_in, b_in.reshape(1, HID), w_out)


def solution(mesh):
    placed = (
        P(("groups", "strip"), "sub", "rep", None),
        P(("groups", "strip"), "sub", "rep", None),
        P(("groups", "strip"), "sub", None),
        P(("groups", "strip"), "sub", None, None),
        P(),
        P(),
        P(),
    )
    return jax.shard_map(
        partial(shards, mesh.shape["strip"], mesh.shape["sub"]),
        mesh=mesh,
        in_specs=placed,
        out_specs=(
            P(("groups", "strip"), "sub", "rep", None),
            P(("groups", "strip"), "sub", "rep", None),
        ),
        check_vma=False,
    )
```

```python
from functools import partial
import math

import jax
import jax.numpy as jnp
from jax import lax
from jax.experimental import pallas as pl
from jax.experimental.pallas import tpu as pltpu
from jax.sharding import PartitionSpec as P

H = 3
MESH = pl.DeviceIdType.MESH
DIRS = ((-1, 0), (1, 0), (0, -1), (0, 1), (-1, -1), (-1, 1), (1, -1), (1, 1))
NONE = 1 << 30
F32 = jnp.float32
BF16 = jnp.bfloat16
NT = (((1,), (1,)), ((), ()))


def gelu_slope(x):
    a = math.sqrt(2.0 / math.pi)
    x2 = x * x
    t = jnp.tanh(a * x * (1.0 + 0.044715 * x2))
    return 0.5 * (1.0 + t) + (0.5 * a) * x * (1.0 - t * t) * (1.0 + (3 * 0.044715) * x2)


def cut(step, count, width, lead):
    if step < 0:
        return 0, width, lead + count
    if step > 0:
        return count - width, width, lead - width
    return 0, count, lead


def read_ids(pad_ref, ids, total_cols):
    rows, picks = ids.shape
    pad_ref[:, :picks] = ids
    flat = pad_ref[...].T
    row = ((flat.astype(F32) + 0.5) * (1.0 / total_cols)).astype(jnp.int32)
    return row, flat - row * total_cols


def kernel(cfg, src_ref, tgt_ref, ids_ref, og_ref, win_ref, bin_ref, wout_ref,
           sg_ref, tg_ref,
           t_ext, s_ext, t32, s32, corr32, pw32, pwx32, oh_e, oh_m, gh, cst, gc, gext,
           cx, id_pad, out32, send_sem, recv_sem, gc_send, gc_recv, local_sem, rep_sem):
    R, CB, PH, C, K, KP, ns, nc = cfg
    J = 128 // KP
    NG = CB // J
    NB = R * CB
    ER, EC = R + 2 * H, CB + 2 * H
    E = ER * EC
    EP = t32.shape[0] // PH
    GC = NG + 2
    SC = GC * J
    G = ER * GC
    HID = win_ref.shape[1]
    inv_root = 1.0 / math.sqrt(C)

    z = lax.axis_index("strip")
    x = lax.axis_index("sub")
    rep = lax.axis_index("rep")
    other = 1 - rep

    def exists(dr, dc):
        ok = jnp.bool_(True)
        if dr < 0:
            ok = jnp.logical_and(ok, z > 0)
        if dr > 0:
            ok = jnp.logical_and(ok, z < ns - 1)
        if dc < 0:
            ok = jnp.logical_and(ok, x > 0)
        if dc > 0:
            ok = jnp.logical_and(ok, x < nc - 1)
        return ok

    def device(dr, dc):
        return {"strip": z + dr, "sub": x + dc}

    barrier = pltpu.get_barrier_semaphore()
    for dr, dc in DIRS:
        @pl.when(exists(dr, dc))
        def _():
            pl.semaphore_signal(barrier, inc=1, device_id=device(dr, dc), device_id_type=MESH)
    pl.semaphore_signal(barrier, inc=1, device_id={"rep": other}, device_id_type=MESH)
    own_t = pltpu.make_async_copy(tgt_ref, t_ext.at[pl.ds(H, R), pl.ds(H, CB)], local_sem.at[0])
    own_t.start()
    own_s = pltpu.make_async_copy(src_ref, s_ext.at[pl.ds(H, R), pl.ds(J, CB)], local_sem.at[1])
    own_s.start()
    rows_n = 1 + (z > 0).astype(jnp.int32) + (z < ns - 1).astype(jnp.int32)
    cols_n = 1 + (x > 0).astype(jnp.int32) + (x < nc - 1).astype(jnp.int32)
    pl.semaphore_wait(barrier, rows_n * cols_n)

    def copy_of(what, d):
        dr, dc = DIRS[d]
        r0, rn, rd = cut(dr, R, H, H)
        if what == 0:
            c0, cn, cd = cut(dc, CB, H, H)
            a, b = tgt_ref.at[pl.ds(r0, rn), pl.ds(c0, cn)], t_ext.at[pl.ds(rd, rn), pl.ds(cd, cn)]
        elif what == 1:
            c0, cn, cd = cut(dc, CB, H, J)
            a, b = src_ref.at[pl.ds(r0, rn), pl.ds(c0, cn)], s_ext.at[pl.ds(rd, rn), pl.ds(cd, cn)]
        else:
            a, b = ids_ref, cx.at[d]
        return pltpu.make_async_remote_copy(
            src_ref=a, dst_ref=b, send_sem=send_sem.at[what, d], recv_sem=recv_sem.at[what, d],
            device_id=device(dr, dc), device_id_type=MESH)

    def gc_copy(d, r):
        dr, dc = DIRS[d]
        r0, rn, rd = cut(dr, R, H, H)
        c0, cn, cd = cut(dc, NG, 1, 1)
        return pltpu.make_async_remote_copy(
            src_ref=gc.at[r, pl.ds(c0, cn)], dst_ref=gext.at[rd + r - r0, pl.ds(cd, cn)],
            send_sem=gc_send.at[d, r], recv_sem=gc_recv.at[d, r],
            device_id=device(dr, dc), device_id_type=MESH)

    def gc_rows(d):
        r0, rn, _ = cut(DIRS[d][0], R, H, H)
        return range(r0, r0 + rn)

    def start(what):
        for d, (dr, dc) in enumerate(DIRS):
            @pl.when(exists(dr, dc))
            def _():
                copy_of(what, d).start()

    def wait_send(what):
        for d, (dr, dc) in enumerate(DIRS):
            @pl.when(exists(dr, dc))
            def _():
                copy_of(what, d).wait_send()

    def wait_recv(what):
        for d, (dr, dc) in enumerate(DIRS):
            @pl.when(exists(-dr, -dc))
            def _():
                copy_of(what, d).wait_recv()

    start(2)
    start(0)

    for d, (dr, dc) in enumerate(DIRS):
        @pl.when(jnp.logical_not(exists(-dr, -dc)))
        def _():
            _, rn, rd = cut(dr, R, H, H)
            _, cn, cd = cut(dc, CB, H, H)
            t_ext[pl.ds(rd, rn), pl.ds(cd, cn)] = jnp.zeros((rn, cn, PH, C), BF16)
            _, cn, cd = cut(dc, CB, H, J)
            s_ext[pl.ds(rd, rn), pl.ds(cd, cn)] = jnp.zeros((rn, cn, PH, C), BF16)
            _, cn, cd = cut(dc, NG, 1, 1)
            gext[pl.ds(rd, rn), pl.ds(cd, cn)] = jnp.zeros((rn, cn, PH, J * KP), BF16)
            cx[d] = jnp.full((R, CB, K), NONE, jnp.int32)
    for c in tuple(range(J - H)) + tuple(range(J + CB + H, SC)):
        s_ext[:, c] = jnp.zeros((ER, PH, C), BF16)
    if EP > E:
        t32[pl.ds(E * PH, (EP - E) * PH), :] = jnp.zeros(((EP - E) * PH, C), F32)

    gh[...] = jnp.zeros_like(gh)
    for r in range(R):
        rows = og_ref[r].astype(F32).reshape(K * CB, og_ref.shape[3]).astype(BF16)
        out = lax.dot_general(rows, wout_ref[...], NT, preferred_element_type=F32)
        for k in range(K):
            piece = out[k * CB:(k + 1) * CB]
            for q in range(HID // 128):
                gh[q, pl.ds(r * CB * KP + k, CB, stride=KP), :] = piece[:, q * 128:(q + 1) * 128]

    id_pad[...] = jnp.full(id_pad.shape, NONE, jnp.int32)
    total_cols = CB * nc
    own_row, own_col = read_ids(id_pad, ids_ref[...].reshape(NB, K), total_cols)
    lane_e = lax.broadcasted_iota(jnp.int32, (KP, EP), 1)
    e_at = (own_row[:KP] - z * R + H) * EC + own_col[:KP] - x * CB + H
    for b in range(NB):
        oh_e[b // J, pl.ds((b % J) * KP, KP), :] = jnp.where(
            lane_e == e_at[:, b:b + 1], 1.0, 0.0).astype(BF16)

    wait_recv(2)
    lane_m = lax.broadcasted_iota(jnp.int32, (KP, J * NB), 1)

    def mark(row, col, r0, rn, rd, c0, cn, cd):
        row_m = row[:KP] - z * R
        col_m = col[:KP] - x * CB
        inside = (row_m >= 0) & (row_m < R) & (col_m >= 0) & (col_m < CB)
        m = jnp.where(inside, row_m * CB + col_m, -J * NB)
        for r in range(rn):
            for h in range(cn):
                for j in range(J):
                    b = (r0 + r) * CB + (c0 + h) * J + j
                    oh_m[(rd + r) * GC + cd + h, pl.ds(j * KP, KP), :] = jnp.where(
                        lane_m == m[:, b:b + 1] + j * NB, 1.0, 0.0).astype(BF16)

    mark(own_row, own_col, 0, R, H, 0, NG, 1)
    for d, (dr, dc) in enumerate(DIRS):
        row, col = read_ids(id_pad, cx[d].reshape(NB, K), total_cols)
        mark(row, col, *cut(dr, R, H, H), *cut(dc, NG, 1, 1))

    own_t.wait()
    own_s.wait()
    wait_send(0)
    start(1)
    wait_recv(0)

    def widen_t(r, _):
        at = pl.multiple_of(r * (EC * PH), EC * PH)
        t32[pl.ds(at, EC * PH), :] = t_ext[r].reshape(EC * PH, C).astype(F32)
        return 0

    lax.fori_loop(0, ER, widen_t, 0)

    def widen_own(r, _):
        at = pl.multiple_of(r * (CB * PH), CB * PH)
        out32[pl.ds(at, CB * PH), :] = s_ext[H + r, pl.ds(J, CB)].reshape(CB * PH, C).astype(F32)
        return 0

    lax.fori_loop(0, R, widen_own, 0)

    def corr_step(p, _):
        s = out32[pl.ds(p, NB, stride=PH), :].astype(BF16)
        t = t32[pl.ds(p, EP, stride=PH), :].astype(BF16)
        full = lax.dot_general(s, t, NT, preferred_element_type=F32) * inv_root
        at = pl.ds(pl.multiple_of(p * NB, NB), NB)
        corr32[0, at, :] = full[:, :128]
        corr32[1, at, :EP - 128] = full[:, 128:]
        return 0

    lax.fori_loop(0, PH, corr_step, 0, unroll=16)

    def swap(r):
        at = pl.ds(r * CB * KP, CB * KP)
        return pltpu.make_async_remote_copy(
            src_ref=cst.at[0, at], dst_ref=cst.at[1, at],
            send_sem=rep_sem.at[0, r], recv_sem=rep_sem.at[1, r],
            device_id={"rep": other}, device_id_type=MESH)

    for b in range(NB):
        at = pl.ds(b, PH, stride=NB)
        lo = corr32[0, at, :].astype(BF16)
        hi = corr32[1, at, :][:, :EP - 128].astype(BF16)
        oh = oh_e[b // J, pl.ds((b % J) * KP, KP), :]
        got = lax.dot_general(oh[:, :128], lo, NT, preferred_element_type=F32)
        got = got + lax.dot_general(oh[:, 128:], hi, NT, preferred_element_type=F32)
        cst[0, pl.ds(b * KP, KP), :] = got.astype(BF16)
        if (b + 1) % CB == 0:
            swap(b // CB).start()

    w_mine = win_ref[pl.ds(pl.multiple_of(rep * PH, PH), PH), :]
    w_other = win_ref[pl.ds(pl.multiple_of(other * PH, PH), PH), :]

    for r in range(R):
        swap(r).wait()
        for h in range(NG):
            at = pl.ds((r * NG + h) * J * KP, J * KP)
            pre = jnp.dot(cst[0, at, :], w_mine, preferred_element_type=F32)
            pre = pre + jnp.dot(cst[1, at, :], w_other, preferred_element_type=F32) + bin_ref[...]
            up = jnp.concatenate([gh[q, at, :] for q in range(HID // 128)], axis=1)
            grad_pre = (up * gelu_slope(pre)).astype(BF16)
            gc[r, h] = lax.dot_general(
                w_mine, grad_pre, NT, preferred_element_type=F32).astype(BF16)
        for d in reversed(range(len(DIRS))):
            if r in gc_rows(d):
                @pl.when(exists(*DIRS[d]))
                def _():
                    gc_copy(d, r).start()

    lane_j = lax.broadcasted_iota(jnp.int32, (PH, J * KP), 1) // KP
    for g in range(R * NG):
        part = gc[g // NG, g % NG]
        stacked = jnp.concatenate(
            [jnp.where(lane_j == j, part, jnp.zeros_like(part)) for j in range(J)], axis=0)
        pw = jnp.dot(stacked, oh_e[g], preferred_element_type=F32).astype(BF16).astype(F32)
        for j in range(J):
            rows = pl.ds(g * J + j, PH, stride=NB)
            piece = pw[j * PH:(j + 1) * PH]
            pw32[0, rows, :] = piece[:, :128]
            pw32[1, rows, :] = jnp.concatenate(
                [piece[:, 128:], jnp.zeros((PH, 256 - EP), F32)], axis=1)

    def source_step(p, _):
        at = pl.ds(pl.multiple_of(p * NB, NB), NB)
        lo = pw32[0, at, :].astype(BF16)
        hi = pw32[1, at, :][:, :EP - 128].astype(BF16)
        t = t32[pl.ds(p, EP, stride=PH), :].astype(BF16)
        out = jnp.dot(lo, t[:128], preferred_element_type=F32)
        out = out + jnp.dot(hi, t[128:], preferred_element_type=F32)
        out32[pl.ds(p, NB, stride=PH), :] = out * inv_root
        return 0

    lax.fori_loop(0, PH, source_step, 0, unroll=16)
    sg_ref[...] = out32[...].astype(BF16).reshape(sg_ref.shape)

    wait_recv(1)

    def widen_s(r, _):
        at = pl.multiple_of(r * (SC * PH), SC * PH)
        s32[pl.ds(at, SC * PH), :] = s_ext[r].reshape(SC * PH, C).astype(F32)
        return 0

    lax.fori_loop(0, ER, widen_s, 0)

    gext[pl.ds(H, R), pl.ds(1, NG)] = gc[...]
    for d, (dr, dc) in enumerate(DIRS):
        @pl.when(exists(-dr, -dc))
        def _():
            for r in gc_rows(d):
                gc_copy(d, r).wait_recv()
    for g in range(G):
        pwx = jnp.dot(gext[g // GC, g % GC], oh_m[g], preferred_element_type=F32)
        pwx32[pl.ds(g, PH, stride=G), :] = pwx.astype(BF16).astype(F32)

    def target_step(p, _):
        w = pwx32[pl.ds(pl.multiple_of(p * G, G), G), :].T.astype(BF16)
        out = jnp.zeros((NB, C), F32)
        for j in range(J):
            s = s32[pl.ds(j * PH + p, G, stride=J * PH), :].astype(BF16)
            out = out + jnp.dot(w[j * NB:(j + 1) * NB], s, preferred_element_type=F32)
        out32[pl.ds(p, NB, stride=PH), :] = out * inv_root
        return 0

    lax.fori_loop(0, PH, target_step, 0, unroll=16)
    tg_ref[...] = out32[...].astype(BF16).reshape(tg_ref.shape)

    wait_send(1)
    wait_send(2)
    for d, (dr, dc) in enumerate(DIRS):
        @pl.when(exists(dr, dc))
        def _():
            for r in gc_rows(d):
                gc_copy(d, r).wait_send()


def shards(ns, nc, source, target, target_ids, out_grad, w_in, b_in, w_out):
    R, CB, PH, C = source.shape
    K = target_ids.shape[2]
    KP = 32
    J = 128 // KP
    NG = CB // J
    NB = R * CB
    HID = w_in.shape[1]
    ER, EC = R + 2 * H, CB + 2 * H
    E = ER * EC
    EP = -(-E // 16) * 16
    GC = NG + 2
    SC = GC * J
    G = ER * GC
    vmem = pl.BlockSpec(memory_space=pltpu.VMEM)
    hbm = pl.BlockSpec(memory_space=pl.ANY)
    cfg = (R, CB, PH, C, K, KP, ns, nc)
    return pl.pallas_call(
        partial(kernel, cfg),
        out_shape=(jax.ShapeDtypeStruct(source.shape, BF16), jax.ShapeDtypeStruct(target.shape, BF16)),
        in_specs=[hbm, hbm, vmem, vmem, vmem, vmem, vmem],
        out_specs=(vmem, vmem),
        scratch_shapes=[
            pltpu.VMEM((ER, EC, PH, C), BF16),
            pltpu.VMEM((ER, SC, PH, C), BF16),
            pltpu.VMEM((EP * PH, C), F32),
            pltpu.VMEM((ER * SC * PH, C), F32),
            pltpu.VMEM((2, PH * NB, 128), F32),
            pltpu.VMEM((2, PH * NB, 128), F32),
            pltpu.VMEM((PH * G, J * NB), F32),
            pltpu.VMEM((R * NG, J * KP, EP), BF16),
            pltpu.VMEM((G, J * KP, J * NB), BF16),
            pltpu.VMEM((HID // 128, NB * KP, 128), F32),
            pltpu.VMEM((2, NB * KP, PH), BF16),
            pltpu.VMEM((R, NG, PH, J * KP), BF16),
            pltpu.VMEM((ER, GC, PH, J * KP), BF16),
            pltpu.VMEM((8, R, CB, K), jnp.int32),
            pltpu.VMEM((NB, 128), jnp.int32),
            pltpu.VMEM((NB * PH, C), F32),
            pltpu.SemaphoreType.DMA((3, 8)),
            pltpu.SemaphoreType.DMA((3, 8)),
            pltpu.SemaphoreType.DMA((8, R)),
            pltpu.SemaphoreType.DMA((8, R)),
            pltpu.SemaphoreType.DMA((2,)),
            pltpu.SemaphoreType.DMA((2, R)),
        ],
        compiler_params=pltpu.CompilerParams(
            collective_id=0, has_side_effects=True, vmem_limit_bytes=56 * 1024 * 1024),
    )(source, target, target_ids, out_grad.transpose(0, 2, 1, 3), w_in, b_in.reshape(1, HID), w_out)


def solution(mesh):
    placed = (
        P(("groups", "strip"), "sub", "rep", None),
        P(("groups", "strip"), "sub", "rep", None),
        P(("groups", "strip"), "sub", None),
        P(("groups", "strip"), "sub", None, None),
        P(),
        P(),
        P(),
    )
    return jax.shard_map(
        partial(shards, mesh.shape["strip"], mesh.shape["sub"]),
        mesh=mesh,
        in_specs=placed,
        out_specs=(
            P(("groups", "strip"), "sub", "rep", None),
            P(("groups", "strip"), "sub", "rep", None),
        ),
        check_vma=False,
    )
```

```python
from functools import partial
import math

import jax
import jax.numpy as jnp
from jax import lax
from jax.experimental import pallas as pl
from jax.experimental.pallas import tpu as pltpu
from jax.sharding import PartitionSpec as P

H = 3
MESH = pl.DeviceIdType.MESH
DIRS = ((-1, 0), (1, 0), (0, -1), (0, 1), (-1, -1), (-1, 1), (1, -1), (1, 1))
NONE = 1 << 30
F32 = jnp.float32
BF16 = jnp.bfloat16
NT = (((1,), (1,)), ((), ()))


def gelu_slope(x):
    a = math.sqrt(2.0 / math.pi)
    x2 = x * x
    t = jnp.tanh(a * x * (1.0 + 0.044715 * x2))
    return 0.5 * (1.0 + t) + (0.5 * a) * x * (1.0 - t * t) * (1.0 + (3 * 0.044715) * x2)


def cut(step, count, width, lead):
    if step < 0:
        return 0, width, lead + count
    if step > 0:
        return count - width, width, lead - width
    return 0, count, lead


def read_ids(pad_ref, ids, total_cols):
    rows, picks = ids.shape
    pad_ref[:, :picks] = ids
    flat = pad_ref[...].T
    row = ((flat.astype(F32) + 0.5) * (1.0 / total_cols)).astype(jnp.int32)
    return row, flat - row * total_cols


def kernel(cfg, src_ref, tgt_ref, ids_ref, og_ref, win_ref, bin_ref, wout_ref,
           sg_ref, tg_ref,
           t_ext, s_ext, t32, s32, corr32, pw32, pwx32, oh_e, oh_m, gh, cst, gc, gext,
           cx, id_pad, out32, send_sem, recv_sem, gc_send, gc_recv, local_sem, rep_sem):
    R, CB, PH, C, K, KP, ns, nc = cfg
    J = 128 // KP
    NG = CB // J
    NB = R * CB
    ER, EC = R + 2 * H, CB + 2 * H
    E = ER * EC
    EP = t32.shape[0] // PH
    GC = NG + 2
    SC = GC * J
    G = ER * GC
    HID = win_ref.shape[1]
    inv_root = 1.0 / math.sqrt(C)

    z = lax.axis_index("strip")
    x = lax.axis_index("sub")
    rep = lax.axis_index("rep")
    other = 1 - rep

    def exists(dr, dc):
        ok = jnp.bool_(True)
        if dr < 0:
            ok = jnp.logical_and(ok, z > 0)
        if dr > 0:
            ok = jnp.logical_and(ok, z < ns - 1)
        if dc < 0:
            ok = jnp.logical_and(ok, x > 0)
        if dc > 0:
            ok = jnp.logical_and(ok, x < nc - 1)
        return ok

    def device(dr, dc):
        return {"strip": z + dr, "sub": x + dc}

    barrier = pltpu.get_barrier_semaphore()
    for dr, dc in DIRS:
        @pl.when(exists(dr, dc))
        def _():
            pl.semaphore_signal(barrier, inc=1, device_id=device(dr, dc), device_id_type=MESH)
    pl.semaphore_signal(barrier, inc=1, device_id={"rep": other}, device_id_type=MESH)
    own_t = pltpu.make_async_copy(tgt_ref, t_ext.at[pl.ds(H, R), pl.ds(H, CB)], local_sem.at[0])
    own_t.start()
    own_s = pltpu.make_async_copy(src_ref, s_ext.at[pl.ds(H, R), pl.ds(J, CB)], local_sem.at[1])
    own_s.start()
    rows_n = 1 + (z > 0).astype(jnp.int32) + (z < ns - 1).astype(jnp.int32)
    cols_n = 1 + (x > 0).astype(jnp.int32) + (x < nc - 1).astype(jnp.int32)
    pl.semaphore_wait(barrier, rows_n * cols_n)

    def copy_of(what, d):
        dr, dc = DIRS[d]
        r0, rn, rd = cut(dr, R, H, H)
        if what == 0:
            c0, cn, cd = cut(dc, CB, H, H)
            a, b = tgt_ref.at[pl.ds(r0, rn), pl.ds(c0, cn)], t_ext.at[pl.ds(rd, rn), pl.ds(cd, cn)]
        elif what == 1:
            c0, cn, cd = cut(dc, CB, H, J)
            a, b = src_ref.at[pl.ds(r0, rn), pl.ds(c0, cn)], s_ext.at[pl.ds(rd, rn), pl.ds(cd, cn)]
        else:
            a, b = ids_ref, cx.at[d]
        return pltpu.make_async_remote_copy(
            src_ref=a, dst_ref=b, send_sem=send_sem.at[what, d], recv_sem=recv_sem.at[what, d],
            device_id=device(dr, dc), device_id_type=MESH)

    def gc_copy(d, r):
        dr, dc = DIRS[d]
        r0, rn, rd = cut(dr, R, H, H)
        c0, cn, cd = cut(dc, NG, 1, 1)
        return pltpu.make_async_remote_copy(
            src_ref=gc.at[r, pl.ds(c0, cn)], dst_ref=gext.at[rd + r - r0, pl.ds(cd, cn)],
            send_sem=gc_send.at[d, r], recv_sem=gc_recv.at[d, r],
            device_id=device(dr, dc), device_id_type=MESH)

    def gc_rows(d):
        r0, rn, _ = cut(DIRS[d][0], R, H, H)
        return range(r0, r0 + rn)

    def start(what):
        for d, (dr, dc) in enumerate(DIRS):
            @pl.when(exists(dr, dc))
            def _():
                copy_of(what, d).start()

    def wait_send(what):
        for d, (dr, dc) in enumerate(DIRS):
            @pl.when(exists(dr, dc))
            def _():
                copy_of(what, d).wait_send()

    def wait_recv(what):
        for d, (dr, dc) in enumerate(DIRS):
            @pl.when(exists(-dr, -dc))
            def _():
                copy_of(what, d).wait_recv()

    start(2)
    start(0)

    for d, (dr, dc) in enumerate(DIRS):
        @pl.when(jnp.logical_not(exists(-dr, -dc)))
        def _():
            _, rn, rd = cut(dr, R, H, H)
            _, cn, cd = cut(dc, CB, H, H)
            t_ext[pl.ds(rd, rn), pl.ds(cd, cn)] = jnp.zeros((rn, cn, PH, C), BF16)
            _, cn, cd = cut(dc, CB, H, J)
            s_ext[pl.ds(rd, rn), pl.ds(cd, cn)] = jnp.zeros((rn, cn, PH, C), BF16)
            _, cn, cd = cut(dc, NG, 1, 1)
            gext[pl.ds(rd, rn), pl.ds(cd, cn)] = jnp.zeros((rn, cn, PH, J * KP), BF16)
            cx[d] = jnp.full((R, CB, K), NONE, jnp.int32)
    for c in tuple(range(J - H)) + tuple(range(J + CB + H, SC)):
        s_ext[:, c] = jnp.zeros((ER, PH, C), BF16)
    if EP > E:
        t32[pl.ds(E * PH, (EP - E) * PH), :] = jnp.zeros(((EP - E) * PH, C), F32)

    gh[...] = jnp.zeros_like(gh)
    for r in range(R):
        rows = og_ref[r].astype(F32).reshape(K * CB, og_ref.shape[3]).astype(BF16)
        out = lax.dot_general(rows, wout_ref[...], NT, preferred_element_type=F32)
        for k in range(K):
            piece = out[k * CB:(k + 1) * CB]
            for q in range(HID // 128):
                gh[q, pl.ds(r * CB * KP + k, CB, stride=KP), :] = piece[:, q * 128:(q + 1) * 128]

    id_pad[...] = jnp.full(id_pad.shape, NONE, jnp.int32)
    total_cols = CB * nc
    own_row, own_col = read_ids(id_pad, ids_ref[...].reshape(NB, K), total_cols)
    lane_e = lax.broadcasted_iota(jnp.int32, (KP, EP), 1)
    e_at = (own_row[:KP] - z * R + H) * EC + own_col[:KP] - x * CB + H
    for b in range(NB):
        oh_e[b // J, pl.ds((b % J) * KP, KP), :] = jnp.where(
            lane_e == e_at[:, b:b + 1], 1.0, 0.0).astype(BF16)

    wait_recv(2)
    lane_m = lax.broadcasted_iota(jnp.int32, (KP, J * NB), 1)

    def mark(row, col, r0, rn, rd, c0, cn, cd):
        row_m = row[:KP] - z * R
        col_m = col[:KP] - x * CB
        inside = (row_m >= 0) & (row_m < R) & (col_m >= 0) & (col_m < CB)
        m = jnp.where(inside, row_m * CB + col_m, -J * NB)
        for r in range(rn):
            for h in range(cn):
                for j in range(J):
                    b = (r0 + r) * CB + (c0 + h) * J + j
                    oh_m[(rd + r) * GC + cd + h, pl.ds(j * KP, KP), :] = jnp.where(
                        lane_m == m[:, b:b + 1] + j * NB, 1.0, 0.0).astype(BF16)

    mark(own_row, own_col, 0, R, H, 0, NG, 1)
    for d, (dr, dc) in enumerate(DIRS):
        row, col = read_ids(id_pad, cx[d].reshape(NB, K), total_cols)
        mark(row, col, *cut(dr, R, H, H), *cut(dc, NG, 1, 1))

    own_t.wait()
    own_s.wait()
    wait_send(0)
    start(1)
    wait_recv(0)

    def widen_t(r, _):
        at = pl.multiple_of(r * (EC * PH), EC * PH)
        t32[pl.ds(at, EC * PH), :] = t_ext[r].reshape(EC * PH, C).astype(F32)
        return 0

    lax.fori_loop(0, ER, widen_t, 0)

    def widen_own(r, _):
        at = pl.multiple_of(r * (CB * PH), CB * PH)
        out32[pl.ds(at, CB * PH), :] = s_ext[H + r, pl.ds(J, CB)].reshape(CB * PH, C).astype(F32)
        return 0

    lax.fori_loop(0, R, widen_own, 0)

    def corr_step(p, _):
        s = out32[pl.ds(p, NB, stride=PH), :].astype(BF16)
        t = t32[pl.ds(p, EP, stride=PH), :].astype(BF16)
        full = lax.dot_general(s, t, NT, preferred_element_type=F32) * inv_root
        at = pl.ds(pl.multiple_of(p * NB, NB), NB)
        corr32[0, at, :] = full[:, :128]
        corr32[1, at, :EP - 128] = full[:, 128:]
        return 0

    lax.fori_loop(0, PH, corr_step, 0, unroll=16)

    def swap(r):
        at = pl.ds(r * CB * KP, CB * KP)
        return pltpu.make_async_remote_copy(
            src_ref=cst.at[0, at], dst_ref=cst.at[1, at],
            send_sem=rep_sem.at[0, r], recv_sem=rep_sem.at[1, r],
            device_id={"rep": other}, device_id_type=MESH)

    for b in range(NB):
        at = pl.ds(b, PH, stride=NB)
        lo = corr32[0, at, :].astype(BF16)
        hi = corr32[1, at, :][:, :EP - 128].astype(BF16)
        oh = oh_e[b // J, pl.ds((b % J) * KP, KP), :]
        got = lax.dot_general(oh[:, :128], lo, NT, preferred_element_type=F32)
        got = got + lax.dot_general(oh[:, 128:], hi, NT, preferred_element_type=F32)
        cst[0, pl.ds(b * KP, KP), :] = got.astype(BF16)
        if (b + 1) % CB == 0:
            swap(b // CB).start()

    w_mine = win_ref[pl.ds(pl.multiple_of(rep * PH, PH), PH), :]
    w_other = win_ref[pl.ds(pl.multiple_of(other * PH, PH), PH), :]

    for r in range(R):
        swap(r).wait()
        for h in range(NG):
            at = pl.ds((r * NG + h) * J * KP, J * KP)
            pre = jnp.dot(cst[0, at, :], w_mine, preferred_element_type=F32)
            pre = pre + jnp.dot(cst[1, at, :], w_other, preferred_element_type=F32) + bin_ref[...]
            up = jnp.concatenate([gh[q, at, :] for q in range(HID // 128)], axis=1)
            grad_pre = (up * gelu_slope(pre)).astype(BF16)
            gc[r, h] = lax.dot_general(
                w_mine, grad_pre, NT, preferred_element_type=F32).astype(BF16)
        for d in reversed(range(len(DIRS))):
            if r in gc_rows(d):
                @pl.when(exists(*DIRS[d]))
                def _():
                    gc_copy(d, r).start()

    lane_j = lax.broadcasted_iota(jnp.int32, (PH, J * KP), 1) // KP
    for g in range(R * NG):
        part = gc[g // NG, g % NG]
        stacked = jnp.concatenate(
            [jnp.where(lane_j == j, part, jnp.zeros_like(part)) for j in range(J)], axis=0)
        pw = jnp.dot(stacked, oh_e[g], preferred_element_type=F32).astype(BF16).astype(F32)
        for j in range(J):
            rows = pl.ds(g * J + j, PH, stride=NB)
            piece = pw[j * PH:(j + 1) * PH]
            pw32[0, rows, :] = piece[:, :128]
            pw32[1, rows, :] = jnp.concatenate(
                [piece[:, 128:], jnp.zeros((PH, 256 - EP), F32)], axis=1)

    def source_step(p, _):
        at = pl.ds(pl.multiple_of(p * NB, NB), NB)
        lo = pw32[0, at, :].astype(BF16)
        hi = pw32[1, at, :][:, :EP - 128].astype(BF16)
        t = t32[pl.ds(p, EP, stride=PH), :].astype(BF16)
        out = jnp.dot(lo, t[:128], preferred_element_type=F32)
        out = out + jnp.dot(hi, t[128:], preferred_element_type=F32)
        out32[pl.ds(p, NB, stride=PH), :] = out * inv_root
        return 0

    lax.fori_loop(0, PH, source_step, 0, unroll=16)
    sg_ref[...] = out32[...].astype(BF16).reshape(sg_ref.shape)

    def pair_weights(g, part):
        pwx = jnp.dot(part, oh_m[g], preferred_element_type=F32)
        pwx32[pl.ds(g, PH, stride=G), :] = pwx.astype(BF16).astype(F32)

    own_groups = [(H + r) * GC + 1 + h for r in range(R) for h in range(NG)]
    for i, g in enumerate(own_groups):
        pair_weights(g, gc[i // NG, i % NG])

    wait_recv(1)

    def widen_s(r, _):
        at = pl.multiple_of(r * (SC * PH), SC * PH)
        s32[pl.ds(at, SC * PH), :] = s_ext[r].reshape(SC * PH, C).astype(F32)
        return 0

    lax.fori_loop(0, ER, widen_s, 0)

    for d, (dr, dc) in enumerate(DIRS):
        @pl.when(exists(-dr, -dc))
        def _():
            for r in gc_rows(d):
                gc_copy(d, r).wait_recv()
    for g in range(G):
        if g not in own_groups:
            pair_weights(g, gext[g // GC, g % GC])

    def target_step(p, _):
        w = pwx32[pl.ds(pl.multiple_of(p * G, G), G), :].T.astype(BF16)
        out = jnp.zeros((NB, C), F32)
        for j in range(J):
            s = s32[pl.ds(j * PH + p, G, stride=J * PH), :].astype(BF16)
            out = out + jnp.dot(w[j * NB:(j + 1) * NB], s, preferred_element_type=F32)
        out32[pl.ds(p, NB, stride=PH), :] = out * inv_root
        return 0

    lax.fori_loop(0, PH, target_step, 0, unroll=32)
    tg_ref[...] = out32[...].astype(BF16).reshape(tg_ref.shape)

    wait_send(1)
    wait_send(2)
    for d, (dr, dc) in enumerate(DIRS):
        @pl.when(exists(dr, dc))
        def _():
            for r in gc_rows(d):
                gc_copy(d, r).wait_send()


def shards(ns, nc, source, target, target_ids, out_grad, w_in, b_in, w_out):
    R, CB, PH, C = source.shape
    K = target_ids.shape[2]
    KP = 32
    J = 128 // KP
    NG = CB // J
    NB = R * CB
    HID = w_in.shape[1]
    ER, EC = R + 2 * H, CB + 2 * H
    E = ER * EC
    EP = -(-E // 16) * 16
    GC = NG + 2
    SC = GC * J
    G = ER * GC
    vmem = pl.BlockSpec(memory_space=pltpu.VMEM)
    hbm = pl.BlockSpec(memory_space=pl.ANY)
    cfg = (R, CB, PH, C, K, KP, ns, nc)
    return pl.pallas_call(
        partial(kernel, cfg),
        out_shape=(jax.ShapeDtypeStruct(source.shape, BF16), jax.ShapeDtypeStruct(target.shape, BF16)),
        in_specs=[hbm, hbm, vmem, vmem, vmem, vmem, vmem],
        out_specs=(vmem, vmem),
        scratch_shapes=[
            pltpu.VMEM((ER, EC, PH, C), BF16),
            pltpu.VMEM((ER, SC, PH, C), BF16),
            pltpu.VMEM((EP * PH, C), F32),
            pltpu.VMEM((ER * SC * PH, C), F32),
            pltpu.VMEM((2, PH * NB, 128), F32),
            pltpu.VMEM((2, PH * NB, 128), F32),
            pltpu.VMEM((PH * G, J * NB), F32),
            pltpu.VMEM((R * NG, J * KP, EP), BF16),
            pltpu.VMEM((G, J * KP, J * NB), BF16),
            pltpu.VMEM((HID // 128, NB * KP, 128), F32),
            pltpu.VMEM((2, NB * KP, PH), BF16),
            pltpu.VMEM((R, NG, PH, J * KP), BF16),
            pltpu.VMEM((ER, GC, PH, J * KP), BF16),
            pltpu.VMEM((8, R, CB, K), jnp.int32),
            pltpu.VMEM((NB, 128), jnp.int32),
            pltpu.VMEM((NB * PH, C), F32),
            pltpu.SemaphoreType.DMA((3, 8)),
            pltpu.SemaphoreType.DMA((3, 8)),
            pltpu.SemaphoreType.DMA((8, R)),
            pltpu.SemaphoreType.DMA((8, R)),
            pltpu.SemaphoreType.DMA((2,)),
            pltpu.SemaphoreType.DMA((2, R)),
        ],
        compiler_params=pltpu.CompilerParams(
            collective_id=0, has_side_effects=True, vmem_limit_bytes=56 * 1024 * 1024),
    )(source, target, target_ids, out_grad.transpose(0, 2, 1, 3), w_in, b_in.reshape(1, HID), w_out)


def solution(mesh):
    placed = (
        P(("groups", "strip"), "sub", "rep", None),
        P(("groups", "strip"), "sub", "rep", None),
        P(("groups", "strip"), "sub", None),
        P(("groups", "strip"), "sub", None, None),
        P(),
        P(),
        P(),
    )
    return jax.shard_map(
        partial(shards, mesh.shape["strip"], mesh.shape["sub"]),
        mesh=mesh,
        in_specs=placed,
        out_specs=(
            P(("groups", "strip"), "sub", "rep", None),
            P(("groups", "strip"), "sub", "rep", None),
        ),
        check_vma=False,
    )
```
